512 devices in a mesh: tm: 8 (over y_hi, x), chan: 64 (over y_lo, z, core).
Axes of the slice: x: 4, y: 4 (y_hi: 2, y_lo: 2; y = y_hi * 2 + y_lo), z: 16, core: 2. Of those that a mesh axis runs over, the one named last changes fastest.
Arguments:
- samples: bfloat16 [2048, 262144], P('chan', 'tm'), may hold values from -144 to 144
- input_map: int32 [2048], replicated, may hold values from 0 to 2047, each once
Outputs:
- visibilities: bfloat16 [64, 2, 2048, 2048], P('chan', None, 'tm')
The draws below stay inside these ranges and needn't reach their ends.
Inputs may be any that keep to these rules, and one draw needn't show every extreme that they name: `input_map`: each of 0 .. 2047 appears once.
All inputs are finite; a program needn't handle non-finite values.
Results may differ from the reference program's by a relative error of at most 0.0069.
Values may be sent and summed in bfloat16 or wider, within the bound.
A program may use at most 64 MiB of HBM per device.

```python
import math
import jax
import jax.numpy as jnp
from jax import lax

NFFT = 8192
NS = 2048
TAPS = 4
CH_SLAB = 64
SLAB_START = 2016
S_TOTAL = 32
TIME = 262144


def level_of(stream_key, dims, cuts, low, largest):
    gain, own = 1.0, jax.random.fold_in(stream_key, 6)
    for axis_at, parts in cuts:
        draws = jnp.exp(jax.random.uniform(jax.random.fold_in(own, axis_at), (parts,), jnp.float32, low / len(cuts), largest / len(cuts)))
        gain = gain * jnp.repeat(draws, dims[axis_at] // parts).reshape([-1 if axis == axis_at else 1 for axis in range(len(dims))])
    return gain


def centred(own_key, extent, width, limit, shards=(), held_as=jnp.bfloat16):
    drawn = width * jax.random.normal(own_key, extent, jnp.float32)
    if shards:
        drawn = drawn * level_of(own_key, extent, shards, -0.22, 0.18)
    return jnp.clip(drawn, -limit, limit).astype(held_as)


def setup_inputs(seed: int = 0) -> dict:
    key_list = jax.random.split(jax.random.key(seed), 3)
    samples = centred(key_list[0], (NS, TIME), 48.0, 144.0, ((0, 64), (1, 8)))
    input_map = jax.random.permutation(key_list[1], NS).astype(jnp.int32)
    return {"samples": samples, "input_map": input_map}


def window_table(frame_len, tap_count, first_channel, channel_count):
    sample_pos = jnp.arange(tap_count * frame_len, dtype=jnp.float32)
    offset = (sample_pos + 0.5 - 0.5 * tap_count * frame_len) / frame_len
    taper = 0.5 - 0.5 * jnp.cos(2.0 * jnp.pi * (sample_pos + 0.5) / (tap_count * frame_len))
    weights = jnp.sinc(offset) * taper / (128.0 * math.sqrt(frame_len))
    per_tap = weights.reshape(tap_count, frame_len).T
    within = jnp.arange(frame_len, dtype=jnp.int32)
    channel_ids = first_channel + jnp.arange(channel_count, dtype=jnp.int32)
    phase = within[:, None] * channel_ids[None, :] % frame_len
    theta = 2.0 * jnp.pi * phase.astype(jnp.float32) / frame_len
    cosine = per_tap[:, :, None] * jnp.cos(theta)[:, None, :]
    sine = -per_tap[:, :, None] * jnp.sin(theta)[:, None, :]
    return jnp.stack([cosine, sine], axis=2).astype(jnp.bfloat16)

def reference(samples, input_map):
    twiddle = window_table(NFFT, TAPS, SLAB_START, CH_SLAB)
    block_count = NS // 64
    blocks = samples.reshape(block_count, 64, S_TOTAL * NFFT)

    def channelize(block):
        voltage = block.astype(jnp.bfloat16)
        padded = jnp.concatenate([jnp.zeros((64, (TAPS - 1) * NFFT), jnp.bfloat16), voltage], axis=1)
        frames = padded.reshape(64, S_TOTAL + TAPS - 1, NFFT).astype(jnp.float32)
        accum = jnp.zeros((S_TOTAL, 2, CH_SLAB, 64), jnp.float32)
        for tap_index in range(TAPS):
            accum = accum + jnp.einsum('afn,nrk->frka', frames[:, tap_index:tap_index + S_TOTAL], twiddle[:, tap_index].astype(jnp.float32), precision=lax.Precision.HIGHEST)
        return accum.astype(jnp.bfloat16)
    spectra = lax.map(channelize, blocks)
    spectra = jnp.moveaxis(spectra, 0, 3).reshape(S_TOTAL, 2, CH_SLAB, NS)
    ordered = jnp.take(spectra, input_map, axis=3)
    by_channel = jnp.moveaxis(ordered, 2, 0)

    def correlate(chan_data):
        real_part = chan_data[:, 0]
        imag_part = chan_data[:, 1]
        stacked = jnp.concatenate([real_part, imag_part], axis=0)
        flipped = jnp.concatenate([imag_part, -real_part], axis=0)
        real_out = jnp.dot(stacked.T, stacked, preferred_element_type=jnp.float32)
        imag_out = jnp.dot(flipped.T, stacked, preferred_element_type=jnp.float32)
        return (jnp.stack([real_out, imag_out]) / S_TOTAL).astype(jnp.bfloat16)
    return lax.map(correlate, by_channel)
```

```python
import functools
import math

import jax
import jax.numpy as jnp
import ml_dtypes
import numpy as np
from jax import lax
from jax.experimental import pallas as pl
from jax.experimental.pallas import tpu as pltpu
from jax.sharding import PartitionSpec as P

NFFT = 8192
TAPS = 4
CHUNK = 1024
PARTS = 2
GROUP = 4
VMEM_BYTES = 61 * 1024 * 1024
GRAM_BYTES = 24 * 1024 * 1024
MESH = pl.DeviceIdType.MESH


def twiddle_table(channel_total):
    first_channel = (NFFT // 2 - channel_total) // 2
    m = np.arange(TAPS * NFFT, dtype=np.float64)
    offset = (m + 0.5 - 0.5 * TAPS * NFFT) / NFFT
    taper = 0.5 - 0.5 * np.cos(2.0 * np.pi * (m + 0.5) / (TAPS * NFFT))
    coefficient = np.sinc(offset) * taper / (128.0 * math.sqrt(NFFT))
    coefficient = coefficient.astype(np.float32).reshape(TAPS, NFFT)
    n = np.arange(NFFT, dtype=np.int64)
    channels = first_channel + np.arange(channel_total, dtype=np.int64)
    theta = 2.0 * np.pi * ((channels[:, None] * n[None, :]) % NFFT) / NFFT
    wave = np.stack([np.cos(theta), -np.sin(theta)], axis=1).astype(np.float32)
    wave = wave.reshape(2, channel_total // 4, 2, 2, NFFT)
    wave = wave.transpose(0, 2, 3, 1, 4).reshape(2 * channel_total, NFFT)
    table = (coefficient[:, None, :] * wave[None]).reshape(-1, NFFT)
    return np.ascontiguousarray(table.T).astype(ml_dtypes.bfloat16)


def turn_kernel(
    n_tm, n_z, x_hbm, tw_hbm, map_hbm, out_ref,
    tw_v, map_ref, xs, acc, own, halo, own_in, halo_in, tiles32, tiles, ring, low_hot,
    tw_sem, map_sem, x_sem, s1_send, s1_recv, h_send, h_recv, z_send, z_recv, t_send, t_recv,
):
    span = NFFT // PARTS
    chunks = span // CHUNK
    half = 2 * 2 * 2 * n_z
    tm = lax.axis_index("tm")
    chan = lax.axis_index("chan")
    y_lo = chan // (2 * n_z)
    z = (chan // 2) % n_z
    core = chan % 2
    group = y_lo * 2 + core

    def chan_of(g, z_at):
        return (g // 2) * (2 * n_z) + z_at * 2 + g % 2

    def load_frames(part):
        return [
            pltpu.make_async_copy(
                x_hbm.at[:, pl.ds(f * NFFT + part * span, span)],
                xs.at[part, f],
                x_sem.at[part, f],
            )
            for f in range(TAPS)
        ]

    def load_table(c):
        at = pl.ds(pl.multiple_of(c * CHUNK, CHUNK), CHUNK)
        return pltpu.make_async_copy(tw_hbm.at[at], tw_v.at[at], tw_sem.at[c])

    for part in range(PARTS):
        for copy in load_frames(part):
            copy.start()
        for c in range(part * chunks, (part + 1) * chunks):
            load_table(c).start()
    signal_map = pltpu.make_async_copy(map_hbm, map_ref, map_sem)
    signal_map.start()

    barrier = pltpu.get_barrier_semaphore()

    def greet(tm_at, chan_at):
        pl.semaphore_signal(
            barrier, inc=1, device_id={"tm": tm_at, "chan": chan_at}, device_id_type=MESH
        )

    next_tm = (tm + 1) % n_tm
    prev_tm = (tm + n_tm - 1) % n_tm
    for e in range(1, GROUP):
        greet(tm, chan_of((group + e) % GROUP, z))
    for e in range(GROUP):
        greet(prev_tm, chan_of((group + e) % GROUP, z))
    for d in range(1, n_z):
        greet(tm, chan_of(group, (z + d) % n_z))
    for e in range(1, n_tm):
        greet((tm + e) % n_tm, chan)

    for part in range(PARTS):
        for copy in load_frames(part):
            copy.wait()
        for i in range(chunks):
            c = part * chunks + i
            load_table(c).wait()
            frames = xs[part, :, :, i * CHUNK : (i + 1) * CHUNK].reshape(TAPS * 32, CHUNK)
            table = tw_v[c * CHUNK : (c + 1) * CHUNK, :]
            product = jnp.dot(frames, table, preferred_element_type=jnp.float32)
            acc[...] = product if c == 0 else acc[...] + product

    def tap_sum(s, taps):
        return sum(
            acc[(s + t) % TAPS * 32 : ((s + t) % TAPS + 1) * 32, t * half : (t + 1) * half]
            for t in taps
        )

    here = [tap_sum(s + 1, range(TAPS - 1 - s, TAPS)) for s in range(TAPS)]
    later = [tap_sum(s + 1, range(TAPS - 1 - s)) for s in range(TAPS - 1)]
    later.append(jnp.zeros_like(later[0]))
    here = jnp.concatenate(here, axis=0).T
    later = jnp.concatenate(later, axis=0).T
    own[...] = here.reshape(GROUP, half // GROUP, 128)
    halo[...] = later.astype(jnp.bfloat16).reshape(GROUP, half // GROUP, 128)

    pl.semaphore_wait(barrier, (GROUP - 1) + GROUP + (n_z - 1) + (n_tm - 1))

    sends = []
    recvs = []
    for e in range(GROUP):
        to = (group + e) % GROUP
        copy = pltpu.make_async_remote_copy(
            src_ref=halo.at[to], dst_ref=halo_in.at[group],
            send_sem=h_send.at[e], recv_sem=h_recv.at[e],
            device_id={"tm": next_tm, "chan": chan_of(to, z)}, device_id_type=MESH,
        )
        copy.start()
        sends.append(copy)
        recvs.append(copy)
    for e in range(1, GROUP):
        to = (group + e) % GROUP
        copy = pltpu.make_async_remote_copy(
            src_ref=own.at[to], dst_ref=own_in.at[group],
            send_sem=s1_send.at[e], recv_sem=s1_recv.at[e],
            device_id={"tm": tm, "chan": chan_of(to, z)}, device_id_type=MESH,
        )
        copy.start()
        sends.append(copy)
        recvs.append(copy)
    own_in[group] = own[group]

    signal_map.wait()
    source = map_ref[...]
    source_z = (source // 64) % n_z
    low_of = (source_z % 2) * 128 + (source // (64 * n_z)) * 64 + source % 64
    pair_of = source_z // 2
    low_row = lax.broadcasted_iota(jnp.int32, (256, 1), 0)
    low_hot[...] = jnp.where(low_row == low_of, 1.0, 0.0).astype(jnp.bfloat16)

    for copy in recvs:
        copy.wait_recv()

    block = lax.broadcasted_iota(jnp.int32, (half // GROUP, 128), 1) // 32
    whole = []
    for g in range(GROUP):
        whole.append(own_in[g] + jnp.where(tm > 0, halo_in[g].astype(jnp.float32), 0.0))
    for s in range(TAPS):
        turned = whole[s]
        for g in range(GROUP):
            if g != s:
                turned = jnp.where(
                    block == g, pltpu.roll(whole[g], ((g - s) % GROUP) * 32, 1), turned
                )
        for r in range(2):
            tiles32[pl.ds(r * TAPS + s, n_z, stride=8), :] = turned[r * n_z : (r + 1) * n_z, :]
    tiles[...] = tiles32[...].reshape(n_z, 8, 128).astype(jnp.bfloat16)

    recvs = []
    for d in sorted(range(1, n_z), key=lambda d: abs(d - n_z // 2)):
        to = (z + d) % n_z
        copy = pltpu.make_async_remote_copy(
            src_ref=tiles.at[to], dst_ref=ring.at[z],
            send_sem=z_send.at[d], recv_sem=z_recv.at[d],
            device_id={"tm": tm, "chan": chan_of(group, to)}, device_id_type=MESH,
        )
        copy.start()
        sends.append(copy)
        recvs.append(copy)
    ring[z] = tiles[z]
    for copy in recvs:
        copy.wait_recv()

    n_pair = n_z // 2
    pairs = ring[...].astype(jnp.float32).reshape(n_pair, 2, 8, 128)
    pairs = jnp.concatenate([pairs[:, 0], pairs[:, 1]], axis=-1)
    pairs = pairs.reshape(n_pair * 8, 256).astype(jnp.bfloat16)
    picked = jnp.dot(pairs, low_hot[...], preferred_element_type=jnp.float32)
    ordered = jnp.zeros((8, n_z * 128), jnp.float32)
    for pair in range(n_pair):
        ordered = ordered + jnp.where(pair_of == pair, picked[pair * 8 : (pair + 1) * 8], 0.0)
    out_ref[tm] = ordered.astype(jnp.bfloat16)

    recvs = []
    for e in sorted(range(1, n_tm), key=lambda e: abs(e - n_tm // 2)):
        copy = pltpu.make_async_remote_copy(
            src_ref=out_ref.at[tm], dst_ref=out_ref.at[tm],
            send_sem=t_send.at[e], recv_sem=t_recv.at[e],
            device_id={"tm": (tm + e) % n_tm, "chan": chan}, device_id_type=MESH,
        )
        copy.start()
        sends.append(copy)
        recvs.append(copy)
    for copy in recvs:
        copy.wait_recv()

    for copy in sends:
        copy.wait_send()


def gram_kernel(n_tm, x_ref, out_hbm, left, blocks, out_sem):
    n_block, _, rows, width = blocks.shape

    def packed(x):
        return x.astype(jnp.float32).reshape(n_tm * 8, x.shape[-1]).astype(jnp.bfloat16)

    start = pl.multiple_of(lax.axis_index("tm") * rows, rows)
    mine = x_ref[:, :, pl.ds(start, rows)].astype(jnp.float32)
    row = lax.broadcasted_iota(jnp.int32, mine.shape, 1)
    other = pltpu.roll(mine, 4, 1)
    flipped = jnp.where(row < 4, other, -other)
    left[:rows, :] = mine.reshape(n_tm * 8, rows).T.astype(jnp.bfloat16)
    left[rows:, :] = flipped.reshape(n_tm * 8, rows).T.astype(jnp.bfloat16)
    copies = []
    for j in range(n_block):
        right = packed(x_ref[:, :, j * width : (j + 1) * width])
        products = jnp.dot(left[...], right, preferred_element_type=jnp.float32)
        products = products * (1.0 / (4 * n_tm))
        blocks[j] = products.reshape(2, rows, width).astype(jnp.bfloat16)
        copy = pltpu.make_async_copy(
            blocks.at[j], out_hbm.at[0, :, :, pl.ds(j * width, width)], out_sem.at[j]
        )
        copy.start()
        copies.append(copy)
    for copy in copies:
        copy.wait()


def shards(n_tm, n_chan, table, samples, input_map):
    n_z = n_chan // 4
    signals = 32 * n_chan
    half = 2 * n_chan
    f32, bf16 = jnp.float32, jnp.bfloat16
    dma = pltpu.SemaphoreType.DMA
    ordered = pl.pallas_call(
        functools.partial(turn_kernel, n_tm, n_z),
        out_shape=pltpu.VMEM((n_tm, 8, signals), bf16),
        in_specs=[
            pl.BlockSpec(memory_space=pltpu.HBM),
            pl.BlockSpec(memory_space=pltpu.HBM),
            pl.BlockSpec(memory_space=pltpu.HBM),
        ],
        out_specs=pl.BlockSpec(memory_space=pltpu.VMEM),
        scratch_shapes=[
            pltpu.VMEM((NFFT, TAPS * half), bf16),
            pltpu.VMEM((1, signals), jnp.int32),
            pltpu.VMEM((PARTS, TAPS, 32, NFFT // PARTS), bf16),
            pltpu.VMEM((TAPS * 32, TAPS * half), f32),
            pltpu.VMEM((GROUP, half // GROUP, 128), f32),
            pltpu.VMEM((GROUP, half // GROUP, 128), bf16),
            pltpu.VMEM((GROUP, half // GROUP, 128), f32),
            pltpu.VMEM((GROUP, half // GROUP, 128), bf16),
            pltpu.VMEM((n_z * 8, 128), f32),
            pltpu.VMEM((n_z, 8, 128), bf16),
            pltpu.VMEM((n_z, 8, 128), bf16),
            pltpu.VMEM((256, signals), bf16),
            dma((NFFT // CHUNK,)),
            dma,
            dma((PARTS, TAPS)),
            dma((GROUP,)),
            dma((GROUP,)),
            dma((GROUP,)),
            dma((GROUP,)),
            dma((n_z,)),
            dma((n_z,)),
            dma((n_tm,)),
            dma((n_tm,)),
        ],
        compiler_params=pltpu.CompilerParams(
            collective_id=0, has_side_effects=True, vmem_limit_bytes=VMEM_BYTES
        ),
        name="turn",
    )(samples, jnp.asarray(table), input_map.reshape(1, signals))
    rows = signals // n_tm
    width = min(256, signals)
    n_block = signals // width
    return pl.pallas_call(
        functools.partial(gram_kernel, n_tm),
        out_shape=jax.ShapeDtypeStruct((1, 2, rows, signals), bf16),
        in_specs=[pl.BlockSpec(memory_space=pltpu.VMEM)],
        out_specs=pl.BlockSpec(memory_space=pl.ANY),
        scratch_shapes=[
            pltpu.VMEM((2 * rows, n_tm * 8), bf16),
            pltpu.VMEM((n_block, 2, rows, width), bf16),
            dma((n_block,)),
        ],
        compiler_params=pltpu.CompilerParams(vmem_limit_bytes=GRAM_BYTES),
        name="gram",
    )(ordered)


def solution(mesh):
    n_tm, n_chan = mesh.shape["tm"], mesh.shape["chan"]
    body = functools.partial(shards, n_tm, n_chan, twiddle_table(n_chan))
    in_specs = (P("chan", "tm"), P())
    out_specs = P("chan", None, "tm", None)
    return jax.shard_map(body, mesh=mesh, in_specs=in_specs, out_specs=out_specs, check_vma=False)
```

```python
import functools
import math

import jax
import jax.numpy as jnp
import ml_dtypes
import numpy as np
from jax import lax
from jax.experimental import pallas as pl
from jax.experimental.pallas import tpu as pltpu
from jax.sharding import PartitionSpec as P

NFFT = 8192
TAPS = 4
PARTS = 4
CHUNKS = (512, 512, 1024, 1024, 1024, 1024, 1024, 1024, 512, 512)
STARTS = tuple(sum(CHUNKS[:c]) for c in range(len(CHUNKS)))
GROUP = 4
VMEM_BYTES = 61 * 1024 * 1024
GRAM_BYTES = 24 * 1024 * 1024
MESH = pl.DeviceIdType.MESH


def twiddle_table(channel_total):
    first_channel = (NFFT // 2 - channel_total) // 2
    m = np.arange(TAPS * NFFT, dtype=np.float64)
    offset = (m + 0.5 - 0.5 * TAPS * NFFT) / NFFT
    taper = 0.5 - 0.5 * np.cos(2.0 * np.pi * (m + 0.5) / (TAPS * NFFT))
    coefficient = np.sinc(offset) * taper / (128.0 * math.sqrt(NFFT))
    coefficient = coefficient.astype(np.float32).reshape(TAPS, NFFT)
    n = np.arange(NFFT, dtype=np.int64)
    channels = first_channel + np.arange(channel_total, dtype=np.int64)
    theta = 2.0 * np.pi * ((channels[:, None] * n[None, :]) % NFFT) / NFFT
    wave = np.stack([np.cos(theta), -np.sin(theta)], axis=1).astype(np.float32)
    wave = wave.reshape(2, channel_total // 4, 2, 2, NFFT)
    wave = wave.transpose(0, 2, 3, 1, 4).reshape(2 * channel_total, NFFT)
    table = (coefficient[:, None, :] * wave[None]).reshape(-1, NFFT)
    return np.ascontiguousarray(table.T).astype(ml_dtypes.bfloat16)


def turn_kernel(
    n_tm, n_z, x_hbm, tw_hbm, map_hbm, out_ref,
    tw_v, map_ref, xs, acc, own, halo, own_in, halo_in, tiles32, tiles, ring, low_hot,
    tw_sem, map_sem, x_sem, s1_send, s1_recv, h_send, h_recv, z_send, z_recv, t_send, t_recv,
):
    span = NFFT // PARTS
    half = 2 * 2 * 2 * n_z
    tm = lax.axis_index("tm")
    chan = lax.axis_index("chan")
    y_lo = chan // (2 * n_z)
    z = (chan // 2) % n_z
    core = chan % 2
    group = y_lo * 2 + core

    def chan_of(g, z_at):
        return (g // 2) * (2 * n_z) + z_at * 2 + g % 2

    def load_frames(part):
        return [
            pltpu.make_async_copy(
                x_hbm.at[:, pl.ds(f * NFFT + part * span, span)],
                xs.at[part, f],
                x_sem.at[part, f],
            )
            for f in range(TAPS)
        ]

    def load_table(c):
        at = pl.ds(STARTS[c], CHUNKS[c])
        return pltpu.make_async_copy(tw_hbm.at[at], tw_v.at[at], tw_sem.at[c])

    frames = [load_frames(part) for part in range(PARTS)]
    tables = [load_table(c) for c in range(len(CHUNKS))]
    signal_map = pltpu.make_async_copy(map_hbm, map_ref, map_sem)
    loads = []
    for c, start in enumerate(STARTS):
        if start % span == 0:
            loads.extend(frames[start // span])
        loads.append(tables[c])
    loads.append(signal_map)
    early = 2 * TAPS + 3
    for copy in loads[:early]:
        copy.start()

    barrier = pltpu.get_barrier_semaphore()

    def greet(tm_at, chan_at):
        pl.semaphore_signal(
            barrier, inc=1, device_id={"tm": tm_at, "chan": chan_at}, device_id_type=MESH
        )

    next_tm = (tm + 1) % n_tm
    prev_tm = (tm + n_tm - 1) % n_tm
    far_z = sorted(range(1, n_z), key=lambda d: abs(d - n_z // 2))
    far_tm = sorted(range(1, n_tm), key=lambda e: abs(e - n_tm // 2))
    for d in far_z:
        greet(tm, chan_of(group, (z + d) % n_z))
    for e in far_tm:
        greet((tm + e) % n_tm, chan)
    for e in range(GROUP):
        greet(prev_tm, chan_of((group + e) % GROUP, z))
    for e in range(1, GROUP):
        greet(tm, chan_of((group + e) % GROUP, z))

    for copy in loads[early:]:
        copy.start()

    for c, start in enumerate(STARTS):
        if start % span == 0:
            for copy in frames[start // span]:
                copy.wait()
        tables[c].wait()
        lanes = slice(start % span, start % span + CHUNKS[c])
        left = xs[start // span, :, :, lanes].reshape(TAPS * 32, CHUNKS[c])
        table = tw_v[start : start + CHUNKS[c], :]
        product = jnp.dot(left, table, preferred_element_type=jnp.float32)
        acc[...] = product if c == 0 else acc[...] + product

    def tap_sum(s, taps):
        return sum(
            acc[(s + t) % TAPS * 32 : ((s + t) % TAPS + 1) * 32, t * half : (t + 1) * half]
            for t in taps
        )

    here = [tap_sum(s + 1, range(TAPS - 1 - s, TAPS)) for s in range(TAPS)]
    later = [tap_sum(s + 1, range(TAPS - 1 - s)) for s in range(TAPS - 1)]
    later.append(jnp.zeros_like(later[0]))
    here = jnp.concatenate(here, axis=0).T
    later = jnp.concatenate(later, axis=0).T
    own[...] = here.reshape(GROUP, half // GROUP, 128)
    halo[...] = later.astype(jnp.bfloat16).reshape(GROUP, half // GROUP, 128)

    pl.semaphore_wait(barrier, (GROUP - 1) + GROUP + (n_z - 1) + (n_tm - 1))

    sends = []
    recvs = []
    for e in range(GROUP):
        to = (group + e) % GROUP
        copy = pltpu.make_async_remote_copy(
            src_ref=halo.at[to], dst_ref=halo_in.at[group],
            send_sem=h_send.at[e], recv_sem=h_recv.at[e],
            device_id={"tm": next_tm, "chan": chan_of(to, z)}, device_id_type=MESH,
        )
        copy.start()
        sends.append(copy)
        recvs.append(copy)
    for e in range(1, GROUP):
        to = (group + e) % GROUP
        copy = pltpu.make_async_remote_copy(
            src_ref=own.at[to], dst_ref=own_in.at[group],
            send_sem=s1_send.at[e], recv_sem=s1_recv.at[e],
            device_id={"tm": tm, "chan": chan_of(to, z)}, device_id_type=MESH,
        )
        copy.start()
        sends.append(copy)
        recvs.append(copy)
    own_in[group] = own[group]

    signal_map.wait()
    source = map_ref[...]
    source_z = (source // 64) % n_z
    low_of = (source_z % 2) * 128 + (source // (64 * n_z)) * 64 + source % 64
    pair_of = source_z // 2
    low_row = lax.broadcasted_iota(jnp.int32, (256, 1), 0)
    low_hot[...] = jnp.where(low_row == low_of, 1.0, 0.0).astype(jnp.bfloat16)

    for copy in recvs:
        copy.wait_recv()

    block = lax.broadcasted_iota(jnp.int32, (half // GROUP, 128), 1) // 32
    whole = []
    for g in range(GROUP):
        whole.append(own_in[g] + jnp.where(tm > 0, halo_in[g].astype(jnp.float32), 0.0))
    for s in range(TAPS):
        turned = whole[s]
        for g in range(GROUP):
            if g != s:
                turned = jnp.where(
                    block == g, pltpu.roll(whole[g], ((g - s) % GROUP) * 32, 1), turned
                )
        for r in range(2):
            tiles32[pl.ds(r * TAPS + s, n_z, stride=8), :] = turned[r * n_z : (r + 1) * n_z, :]
    tiles[...] = tiles32[...].reshape(n_z, 8, 128).astype(jnp.bfloat16)

    recvs = []
    for d in far_z:
        to = (z + d) % n_z
        copy = pltpu.make_async_remote_copy(
            src_ref=tiles.at[to], dst_ref=ring.at[z],
            send_sem=z_send.at[d], recv_sem=z_recv.at[d],
            device_id={"tm": tm, "chan": chan_of(group, to)}, device_id_type=MESH,
        )
        copy.start()
        sends.append(copy)
        recvs.append(copy)
    ring[z] = tiles[z]
    for copy in recvs:
        copy.wait_recv()

    n_pair = n_z // 2
    pairs = ring[...].astype(jnp.float32).reshape(n_pair, 2, 8, 128)
    pairs = jnp.concatenate([pairs[:, 0], pairs[:, 1]], axis=-1)
    pairs = pairs.reshape(n_pair * 8, 256).astype(jnp.bfloat16)
    picked = jnp.dot(pairs, low_hot[...], preferred_element_type=jnp.float32)
    ordered = jnp.zeros((8, n_z * 128), jnp.float32)
    for pair in range(n_pair):
        ordered = ordered + jnp.where(pair_of == pair, picked[pair * 8 : (pair + 1) * 8], 0.0)
    out_ref[tm] = ordered.astype(jnp.bfloat16)

    recvs = []
    for e in far_tm:
        copy = pltpu.make_async_remote_copy(
            src_ref=out_ref.at[tm], dst_ref=out_ref.at[tm],
            send_sem=t_send.at[e], recv_sem=t_recv.at[e],
            device_id={"tm": (tm + e) % n_tm, "chan": chan}, device_id_type=MESH,
        )
        copy.start()
        sends.append(copy)
        recvs.append(copy)
    for copy in recvs:
        copy.wait_recv()

    for copy in sends:
        copy.wait_send()


def gram_kernel(n_tm, x_ref, out_hbm, left, blocks, out_sem):
    n_block, _, rows, width = blocks.shape

    def packed(x):
        return x.astype(jnp.float32).reshape(n_tm * 8, x.shape[-1]).astype(jnp.bfloat16)

    start = pl.multiple_of(lax.axis_index("tm") * rows, rows)
    mine = x_ref[:, :, pl.ds(start, rows)].astype(jnp.float32)
    row = lax.broadcasted_iota(jnp.int32, mine.shape, 1)
    other = pltpu.roll(mine, 4, 1)
    flipped = jnp.where(row < 4, other, -other)
    left[:rows, :] = mine.reshape(n_tm * 8, rows).T.astype(jnp.bfloat16)
    left[rows:, :] = flipped.reshape(n_tm * 8, rows).T.astype(jnp.bfloat16)
    copies = []
    for j in range(n_block):
        right = packed(x_ref[:, :, j * width : (j + 1) * width])
        products = jnp.dot(left[...], right, preferred_element_type=jnp.float32)
        products = products * (1.0 / (4 * n_tm))
        blocks[j] = products.reshape(2, rows, width).astype(jnp.bfloat16)
        copy = pltpu.make_async_copy(
            blocks.at[j], out_hbm.at[0, :, :, pl.ds(j * width, width)], out_sem.at[j]
        )
        copy.start()
        copies.append(copy)
    for copy in copies:
        copy.wait()


def shards(n_tm, n_chan, table, samples, input_map):
    n_z = n_chan // 4
    signals = 32 * n_chan
    half = 2 * n_chan
    f32, bf16 = jnp.float32, jnp.bfloat16
    dma = pltpu.SemaphoreType.DMA
    ordered = pl.pallas_call(
        functools.partial(turn_kernel, n_tm, n_z),
        out_shape=pltpu.VMEM((n_tm, 8, signals), bf16),
        in_specs=[
            pl.BlockSpec(memory_space=pltpu.HBM),
            pl.BlockSpec(memory_space=pltpu.HBM),
            pl.BlockSpec(memory_space=pltpu.HBM),
        ],
        out_specs=pl.BlockSpec(memory_space=pltpu.VMEM),
        scratch_shapes=[
            pltpu.VMEM((NFFT, TAPS * half), bf16),
            pltpu.VMEM((1, signals), jnp.int32),
            pltpu.VMEM((PARTS, TAPS, 32, NFFT // PARTS), bf16),
            pltpu.VMEM((TAPS * 32, TAPS * half), f32),
            pltpu.VMEM((GROUP, half // GROUP, 128), f32),
            pltpu.VMEM((GROUP, half // GROUP, 128), bf16),
            pltpu.VMEM((GROUP, half // GROUP, 128), f32),
            pltpu.VMEM((GROUP, half // GROUP, 128), bf16),
            pltpu.VMEM((n_z * 8, 128), f32),
            pltpu.VMEM((n_z, 8, 128), bf16),
            pltpu.VMEM((n_z, 8, 128), bf16),
            pltpu.VMEM((256, signals), bf16),
            dma((len(CHUNKS),)),
            dma,
            dma((PARTS, TAPS)),
            dma((GROUP,)),
            dma((GROUP,)),
            dma((GROUP,)),
            dma((GROUP,)),
            dma((n_z,)),
            dma((n_z,)),
            dma((n_tm,)),
            dma((n_tm,)),
        ],
        compiler_params=pltpu.CompilerParams(
            collective_id=0, has_side_effects=True, vmem_limit_bytes=VMEM_BYTES
        ),
        name="turn",
    )(samples, jnp.asarray(table), input_map.reshape(1, signals))
    rows = signals // n_tm
    width = min(512, signals)
    n_block = signals // width
    return pl.pallas_call(
        functools.partial(gram_kernel, n_tm),
        out_shape=jax.ShapeDtypeStruct((1, 2, rows, signals), bf16),
        in_specs=[pl.BlockSpec(memory_space=pltpu.VMEM)],
        out_specs=pl.BlockSpec(memory_space=pl.ANY),
        scratch_shapes=[
            pltpu.VMEM((2 * rows, n_tm * 8), bf16),
            pltpu.VMEM((n_block, 2, rows, width), bf16),
            dma((n_block,)),
        ],
        compiler_params=pltpu.CompilerParams(vmem_limit_bytes=GRAM_BYTES),
        name="gram",
    )(ordered)


def solution(mesh):
    n_tm, n_chan = mesh.shape["tm"], mesh.shape["chan"]
    body = functools.partial(shards, n_tm, n_chan, twiddle_table(n_chan))
    in_specs = (P("chan", "tm"), P())
    out_specs = P("chan", None, "tm", None)
    return jax.shard_map(body, mesh=mesh, in_specs=in_specs, out_specs=out_specs, check_vma=False)
```
